32 devices in a mesh: blk: 8 (over z, y), smp: 4 (over x, core).
Axes of the slice: x: 2, y: 2, z: 4, core: 2. Of those that a mesh axis runs over, the one named last changes fastest.
Arguments:
- genotype: bfloat16 [32768, 4096], P('smp', 'blk'), may hold values from -7 to 7
- presence: int32 [6, 4096], P(None, 'blk'), may hold values 0 or 1
- cohort_id: int32 [32768], P('smp'), may hold values from 0 to 5, as said below
- fold_id: int32 [32768], P('smp'), may hold values from 0 to 4
- phenotype: int32 [32768], P('smp'), may hold values from 0 to 1
Outputs:
- level_one: float32 [40], replicated
- linear_pred: float32 [32768], P(('smp', 'blk'))
The draws below stay inside these ranges and needn't reach their ends.
Inputs may be any that keep to these rules, and one draw needn't show every extreme that they name: Samples are laid out by cohort: cohort_id never falls from one sample to the next.
All inputs are finite; a program needn't handle non-finite values. No bound on the sum of `presence` on one device may be relied on, other than what follows from the above.
Results may differ from the reference program's by a relative error of at most 0.0023.
Values sent between devices are 32-bit elements; how exact they have to be, the bound alone decides.
A program may use at most 128 MiB of HBM per device.

```python
import math
import jax
import jax.numpy as jnp
from jax import lax

BS = 512
COHORTS = 6
FOLDS = 5
NEWTON = 4
RIDGE_STEPS = 6
SAMPLES = 32768
BLOCKS = 8
SNPS = 4096
PRED = 40


def shared_cohort(key):
    key = jax.random.fold_in(key, 11)
    inner = jax.random.randint(key, (SAMPLES - 2,), 0, COHORTS, dtype=jnp.int32)
    ends = jnp.array([0, COHORTS - 1], jnp.int32)
    return jnp.sort(jnp.concatenate([ends, inner]))


def shared_trait(key):
    key = jax.random.fold_in(key, 12)
    return jax.random.randint(key, (SAMPLES,), 0, 2, dtype=jnp.int32)


def cohort_factor(key):
    key = jax.random.fold_in(key, 13)
    order = jax.random.permutation(key, COHORTS)
    return 0.5 + 0.25 * order.astype(jnp.float32)


def draw_cohort_id(key, part):
    return shared_cohort(key)


def draw_phenotype(key, part):
    return shared_trait(key)


def draw_genotype(key, part):
    signed = 2.0 * shared_trait(key).astype(jnp.float32) - 1.0
    factor_table = cohort_factor(key)
    cohorts = shared_cohort(key)
    onehot = (cohorts[:, None] == jnp.arange(COHORTS, dtype=jnp.int32)[None, :]).astype(jnp.float32)
    per_sample = jnp.sum(onehot * factor_table[None, :], axis=1)
    key = jax.random.fold_in(key, 7)
    noise_key, effect_key = jax.random.split(key)
    effect = jax.random.truncated_normal(effect_key, -3.0, 3.0, (SNPS,), jnp.float32)
    noise = jax.random.truncated_normal(noise_key, -6.0, 6.0, (SAMPLES, SNPS), jnp.float32)
    strength = math.sqrt(2.0 / BS)
    values = noise + strength * (per_sample * signed)[:, None] * effect[None, :]
    return jnp.clip(values, -7.0, 7.0).astype(jnp.bfloat16)


def touch_ends(values, stream_key, low, high):
    longest = values.shape.index(max(values.shape))
    spots = []
    for shift in (0, 1):
        where = [jax.random.randint(jax.random.fold_in(stream_key, axis), (), 0, length) for axis, length in enumerate(values.shape)]
        where[longest] = (where[longest] + shift) % values.shape[longest]
        spots.append(tuple(where))
    return values.at[spots[0]].set(low).at[spots[1]].set(high)


def setup_inputs(seed: int = 0) -> dict:
    seeds = jax.random.split(jax.random.key(seed), 6)
    genotype = draw_genotype(jax.random.fold_in(seeds[5], 71), 0)
    presence = touch_ends((jax.random.randint(seeds[1], (COHORTS, SNPS), 0, 5) < 4).astype(jnp.int32), jax.random.fold_in(seeds[1], 1), 0, 1)
    cohort_id = draw_cohort_id(jax.random.fold_in(seeds[5], 71), 0)
    fold_id = touch_ends(jax.random.randint(seeds[3], (SAMPLES,), 0, FOLDS), jax.random.fold_in(seeds[3], 1), 0, FOLDS - 1).astype(jnp.int32)
    phenotype = draw_phenotype(jax.random.fold_in(seeds[5], 71), 0)
    return {"genotype": genotype, "presence": presence, "cohort_id": cohort_id, "fold_id": fold_id, "phenotype": phenotype}


penalty_list = (0.002, 0.01, 0.05, 0.25, 1.25)
level_ridge = 0.05

def ridge_solve(gram, cross, shifts, steps):
    high = lax.Precision.HIGHEST
    residual = jnp.broadcast_to(cross[None, :], (shifts.shape[0], cross.shape[0])).astype(jnp.float32)
    solution = jnp.zeros_like(residual)
    direction = residual
    norm_now = lax.optimization_barrier(jnp.sum(residual * residual, axis=1))
    for ridge_step in range(steps):
        image = jnp.dot(direction, gram, precision=high) + shifts[:, None] * direction
        alpha = norm_now / lax.optimization_barrier(jnp.sum(direction * image, axis=1))
        solution = solution + alpha[:, None] * direction
        residual = residual - alpha[:, None] * image
        norm_next = lax.optimization_barrier(jnp.sum(residual * residual, axis=1))
        direction = residual + (norm_next / norm_now)[:, None] * direction
        norm_now = norm_next
    return solution

def block_scores(block_index, genotype, presence, cohort_id, train, target):
    start = (block_index * BS).astype(jnp.int32)
    columns = lax.dynamic_slice_in_dim(genotype, start, BS, 1)
    present_cols = lax.dynamic_slice_in_dim(presence, start, BS, 1)
    onehot = (cohort_id[:, None] == jnp.arange(COHORTS, dtype=jnp.int32)[None, :]).astype(jnp.bfloat16)
    present_rows = jnp.dot(onehot.astype(jnp.float32), present_cols.astype(jnp.bfloat16).astype(jnp.float32), preferred_element_type=jnp.float32).astype(jnp.bfloat16)
    masked = columns * present_rows
    weighted = masked * train.astype(jnp.bfloat16)[:, None]
    gram = lax.dot_general(weighted.astype(jnp.float32), masked.astype(jnp.float32), (((0,), (0,)), ((), ())), preferred_element_type=jnp.float32)
    cross = jnp.dot((train * target).astype(jnp.bfloat16).astype(jnp.float32), masked.astype(jnp.float32), preferred_element_type=jnp.float32)
    shifts = jnp.array([penalty * SAMPLES for penalty in penalty_list], jnp.float32)
    ridge = ridge_solve(gram, cross, shifts, RIDGE_STEPS).astype(jnp.bfloat16)
    scores = lax.dot_general(ridge.astype(jnp.float32), masked.astype(jnp.float32), (((1,), (1,)), ((), ())), preferred_element_type=jnp.float32)
    return scores * jnp.sqrt(jnp.float32(SAMPLES) / BS)

def reference(genotype, presence, cohort_id, fold_id, phenotype):
    train = (fold_id != 0).astype(jnp.float32)
    target = 2.0 * phenotype.astype(jnp.float32) - 1.0
    all_scores = lax.map(lambda block_index: block_scores(block_index, genotype, presence, cohort_id, train, target), jnp.arange(BLOCKS, dtype=jnp.int32))
    scores = all_scores.reshape(PRED, SAMPLES)
    labels = phenotype.astype(jnp.float32)
    level_one = jnp.zeros((PRED,), jnp.float32)
    identity = jnp.eye(PRED, dtype=jnp.float32)
    high = lax.Precision.HIGHEST
    for newton_step in range(NEWTON):
        linear = jnp.dot(level_one, scores, precision=high)
        prob = jax.nn.sigmoid(linear)
        resid = train * (labels - prob)
        curve = train * prob * (1.0 - prob)
        grad = jnp.dot(scores, resid, precision=high)
        hess = lax.dot_general(scores * curve[None, :], scores, (((1,), (1,)), ((), ())), precision=high)
        factor = jnp.linalg.cholesky(hess + level_ridge * SAMPLES * identity)
        level_one = level_one + jax.scipy.linalg.cho_solve((factor, True), grad - level_ridge * SAMPLES * level_one)
    linear_pred = jnp.dot(level_one, scores, precision=high)
    return (level_one, linear_pred)
```

```python
import functools

import jax
import jax.numpy as jnp
from jax import lax
from jax.experimental import pallas as pl
from jax.experimental.pallas import tpu as pltpu
from jax.sharding import PartitionSpec as P

NEWTON = 4
RIDGE_STEPS = 6
PANEL = 8
LANES = 128
MESH = pl.DeviceIdType.MESH


penalty_list = (0.002, 0.01, 0.05, 0.25, 1.25)
level_ridge = 0.05


def ridge_solve(gram, cross, shifts, steps):
    high = lax.Precision.HIGHEST
    residual = jnp.broadcast_to(cross[None, :], (shifts.shape[0], cross.shape[0]))
    solution = jnp.zeros_like(residual)
    direction = residual
    norm_now = jnp.sum(residual * residual, axis=1)
    for ridge_step in range(steps):
        image = jnp.dot(direction, gram, precision=high) + shifts[:, None] * direction
        alpha = norm_now / jnp.sum(direction * image, axis=1)
        solution = solution + alpha[:, None] * direction
        residual = residual - alpha[:, None] * image
        norm_next = jnp.sum(residual * residual, axis=1)
        direction = residual + (norm_next / norm_now)[:, None] * direction
        norm_now = norm_next
    return solution


def low_part(value):
    return value - value.astype(jnp.bfloat16).astype(jnp.float32)


def spd_solve(system, order):
    width = system.shape[1]
    row_of = lax.broadcasted_iota(jnp.int32, (order, width), 0)
    row_of_lane = lax.broadcasted_iota(jnp.int32, (order, LANES), 0)
    for start in range(0, order, PANEL):
        stop = min(start + PANEL, order)
        columns = [
            jnp.broadcast_to(system[:, j : j + 1], (order, LANES)) for j in range(start, stop)
        ]
        for j in range(start, stop):
            column = columns[j - start]
            inverse = 1.0 / column[j : j + 1, :]
            pivot_row = system[j : j + 1, :] * jnp.concatenate(
                [inverse] * pl.cdiv(width, LANES), axis=1
            )[:, :width]
            wide = jnp.concatenate([column] * pl.cdiv(width, LANES), axis=1)[:, :width]
            system = jnp.where(row_of == j, pivot_row, system - wide * pivot_row)
            for k in range(j + 1, stop):
                other = columns[k - start]
                entry = other[j : j + 1, :] * inverse
                columns[k - start] = jnp.where(row_of_lane == j, entry, other - column * entry)
    return jnp.broadcast_to(system[:, order : order + 1], (order, LANES))


def exchange(ref, mine, axis, count, send_sem, recv_sem):
    copies = []
    for distance in range(1, count):
        copy = pltpu.make_async_remote_copy(
            src_ref=ref.at[mine],
            dst_ref=ref.at[mine],
            send_sem=send_sem.at[distance],
            recv_sem=recv_sem.at[distance],
            device_id={axis: lax.rem(mine + distance, count)},
            device_id_type=MESH,
        )
        copy.start()
        copies.append(copy)
    for copy in copies:
        copy.wait_recv()
    total = ref[0]
    for slot in range(1, count):
        total = total + ref[slot]
    for copy in copies:
        copy.wait_send()
    return total


def level_one_kernel(
    blk, smp, total_samples,
    scores_ref, fold_ref, pheno_ref, level_ref, linear_ref,
    gathered, packed, pieces, smp_part, blk_part,
    score_send, score_recv, smp_send, smp_recv, blk_send, blk_recv,
):
    mine_b = lax.axis_index("blk")
    mine_s = lax.axis_index("smp")
    per_block = scores_ref.shape[0]
    owned = packed.shape[1]
    predictors = packed.shape[0]
    barrier = pltpu.get_barrier_semaphore()
    for distance in range(1, blk):
        pl.semaphore_signal(
            barrier, inc=1, device_id={"blk": lax.rem(mine_b + distance, blk)}, device_id_type=MESH
        )
    for distance in range(1, smp):
        pl.semaphore_signal(
            barrier, inc=1, device_id={"smp": lax.rem(mine_s + distance, smp)}, device_id_type=MESH
        )
    pl.semaphore_wait(barrier, blk + smp - 2)

    copies = []
    for distance in range(1, blk):
        target = lax.rem(mine_b + distance, blk)
        copy = pltpu.make_async_remote_copy(
            src_ref=scores_ref.at[:, pl.ds(pl.multiple_of(target * owned, LANES), owned)],
            dst_ref=gathered.at[mine_b],
            send_sem=score_send.at[distance],
            recv_sem=score_recv.at[distance],
            device_id={"blk": target},
            device_id_type=MESH,
        )
        copy.start()
        copies.append(copy)
    own = pl.ds(pl.multiple_of(mine_b * owned, LANES), owned)
    gathered[mine_b] = scores_ref[:, own]
    labels = pheno_ref[:, own].astype(jnp.float32)
    train = (fold_ref[:, own] != 0).astype(jnp.float32)
    for copy in copies:
        copy.wait_recv()
    for block in range(blk):
        packed[block * per_block : (block + 1) * per_block, :] = gathered[block]
    scores = packed[...]
    pieces[...] = jnp.concatenate([scores, low_part(scores)], axis=0).astype(jnp.bfloat16)
    for copy in copies:
        copy.wait_send()

    width = predictors + 8
    pad_row = lax.broadcasted_iota(jnp.int32, (8, owned), 0)
    row_of = lax.broadcasted_iota(jnp.int32, (predictors, width), 0)
    column_of = lax.broadcasted_iota(jnp.int32, (predictors, width), 1)
    ridge = level_ridge * total_samples

    def predict(level):
        return jnp.sum(
            packed[...] * jnp.concatenate([level] * (owned // LANES), axis=1), axis=0, keepdims=True
        )

    def widen(level):
        return jnp.concatenate([level] * pl.cdiv(width, LANES), axis=1)[:, :width]

    def newton(step, level):
        prob = jax.nn.sigmoid(predict(level))
        resid = train * (labels - prob)
        curve = train * prob * (1.0 - prob)
        right = jnp.concatenate(
            [packed[...] * curve, jnp.where(pad_row == 0, resid, 0.0)], axis=0
        )
        moments = jnp.zeros((2 * predictors, width), jnp.float32)
        for part in (right, low_part(right)):
            moments = moments + lax.dot_general(
                pieces[...], part.astype(jnp.bfloat16), (((1,), (1,)), ((), ())),
                preferred_element_type=jnp.float32,
            )
        smp_part[step, mine_s] = moments[:predictors] + moments[predictors:]
        over_smp = exchange(
            smp_part.at[step], mine_s, "smp", smp, smp_send.at[step], smp_recv.at[step]
        )
        blk_part[step, mine_b] = over_smp
        system = exchange(
            blk_part.at[step], mine_b, "blk", blk, blk_send.at[step], blk_recv.at[step]
        )
        system = jnp.where(row_of == column_of, system + ridge, system)
        system = jnp.where(column_of == predictors, system - ridge * widen(level), system)
        return level + spd_solve(system, predictors)

    level = lax.fori_loop(0, NEWTON, newton, jnp.zeros((predictors, LANES), jnp.float32))
    linear_ref[...] = predict(level)
    diagonal = row_of == column_of
    level_ref[...] = jnp.sum(jnp.where(diagonal, widen(level), 0.0), axis=0, keepdims=True)[
        :, :predictors
    ]


def level_one_fit(scores, fold_id, phenotype, total_samples):
    blk = lax.axis_size("blk")
    smp = lax.axis_size("smp")
    per_block, local_count = scores.shape
    owned = local_count // blk
    predictors = per_block * blk
    width = predictors + 8
    dma = pltpu.SemaphoreType.DMA
    level, linear = pl.pallas_call(
        functools.partial(level_one_kernel, blk, smp, total_samples),
        out_shape=(
            jax.ShapeDtypeStruct((1, predictors), jnp.float32),
            jax.ShapeDtypeStruct((1, owned), jnp.float32),
        ),
        in_specs=[pl.BlockSpec(memory_space=pltpu.VMEM)] * 3,
        out_specs=(pl.BlockSpec(memory_space=pltpu.VMEM),) * 2,
        scratch_shapes=[
            pltpu.VMEM((blk, per_block, owned), jnp.float32),
            pltpu.VMEM((predictors, owned), jnp.float32),
            pltpu.VMEM((2 * predictors, owned), jnp.bfloat16),
            pltpu.VMEM((NEWTON, smp, predictors, width), jnp.float32),
            pltpu.VMEM((NEWTON, blk, predictors, width), jnp.float32),
            dma((blk,)), dma((blk,)),
            dma((NEWTON, smp)), dma((NEWTON, smp)),
            dma((NEWTON, blk)), dma((NEWTON, blk)),
        ],
        compiler_params=pltpu.CompilerParams(
            collective_id=0, has_side_effects=True, vmem_limit_bytes=48 * 1024 * 1024
        ),
    )(scores, fold_id.reshape(1, -1), phenotype.reshape(1, -1))
    return level.reshape(predictors), linear.reshape(owned)


def on_device(genotype, presence, cohort_id, fold_id, phenotype):
    local_count = genotype.shape[0]
    width = genotype.shape[1]
    total_samples = local_count * lax.axis_size("smp")
    train = (fold_id != 0).astype(jnp.float32)
    target = 2.0 * phenotype.astype(jnp.float32) - 1.0
    onehot = (cohort_id[:, None] == jnp.arange(presence.shape[0], dtype=jnp.int32)[None, :]).astype(
        jnp.bfloat16
    )
    present_rows = jnp.dot(
        onehot, presence.astype(jnp.bfloat16), preferred_element_type=jnp.float32
    ).astype(jnp.bfloat16)
    masked = genotype * present_rows
    weighted = masked * train.astype(jnp.bfloat16)[:, None]
    gram = lax.dot_general(
        weighted, masked, (((0,), (0,)), ((), ())), preferred_element_type=jnp.float32
    )
    cross = jnp.dot(
        (train * target).astype(jnp.bfloat16), masked, preferred_element_type=jnp.float32
    )
    gram, cross = lax.psum((gram, cross), "smp")
    shifts = jnp.array([penalty * total_samples for penalty in penalty_list], jnp.float32)
    ridge = ridge_solve(gram, cross, shifts, RIDGE_STEPS).astype(jnp.bfloat16)
    scores = lax.dot_general(
        ridge, masked, (((1,), (1,)), ((), ())), preferred_element_type=jnp.float32
    )
    scores = scores * jnp.sqrt(jnp.float32(total_samples) / width)
    return level_one_fit(scores, fold_id, phenotype, total_samples)


def solution(mesh):
    in_specs = (P("smp", "blk"), P(None, "blk"), P("smp"), P("smp"), P("smp"))
    out_specs = (P(), P(("smp", "blk")))
    return jax.shard_map(
        on_device, mesh=mesh, in_specs=in_specs, out_specs=out_specs, check_vma=False
    )
```

```python
import functools

import jax
import jax.numpy as jnp
from jax import lax
from jax.experimental import pallas as pl
from jax.experimental.pallas import tpu as pltpu
from jax.sharding import PartitionSpec as P

NEWTON = 4
RIDGE_STEPS = 6
PANEL = 8
LANES = 128
TILE = 256
PARTS = 7
CHUNK = 1024
MESH = pl.DeviceIdType.MESH


penalty_list = (0.002, 0.01, 0.05, 0.25, 1.25)
level_ridge = 0.05


def low_part(value):
    return value - value.astype(jnp.bfloat16).astype(jnp.float32)


def spd_solve(system, order):
    width = system.shape[1]
    row_of = lax.broadcasted_iota(jnp.int32, (order, width), 0)
    row_of_lane = lax.broadcasted_iota(jnp.int32, (order, LANES), 0)
    for start in range(0, order, PANEL):
        stop = min(start + PANEL, order)
        columns = [
            jnp.broadcast_to(system[:, j : j + 1], (order, LANES)) for j in range(start, stop)
        ]
        for j in range(start, stop):
            column = columns[j - start]
            inverse = 1.0 / column[j : j + 1, :]
            pivot_row = system[j : j + 1, :] * jnp.concatenate(
                [inverse] * pl.cdiv(width, LANES), axis=1
            )[:, :width]
            wide = jnp.concatenate([column] * pl.cdiv(width, LANES), axis=1)[:, :width]
            system = jnp.where(row_of == j, pivot_row, system - wide * pivot_row)
            for k in range(j + 1, stop):
                other = columns[k - start]
                entry = other[j : j + 1, :] * inverse
                columns[k - start] = jnp.where(row_of_lane == j, entry, other - column * entry)
    return jnp.broadcast_to(system[:, order : order + 1], (order, LANES))


def exchange(ref, mine, axis, count, send_sem, recv_sem):
    copies = []
    for distance in range(1, count):
        copy = pltpu.make_async_remote_copy(
            src_ref=ref.at[mine],
            dst_ref=ref.at[mine],
            send_sem=send_sem.at[distance],
            recv_sem=recv_sem.at[distance],
            device_id={axis: lax.rem(mine + distance, count)},
            device_id_type=MESH,
        )
        copy.start()
        copies.append(copy)
    for copy in copies:
        copy.wait_recv()
    total = ref[0]
    for slot in range(1, count):
        total = total + ref[slot]
    for copy in copies:
        copy.wait_send()
    return total


def gram_rows(width):
    return sum(stop + 8 for stop in range(TILE, width + 1, TILE))


def accumulate_gram(chunk, chunks, load, geno, pres, cohort_ref, fold_ref, pheno_ref, gram):
    width = geno.shape[1]
    cohorts = lax.broadcasted_iota(jnp.int32, (pres.shape[0], chunk), 0)
    gram[...] = jnp.zeros_like(gram)

    def body(index, _):
        load(index).wait()
        rows = pl.ds(pl.multiple_of(index * chunk, chunk), chunk)
        train = fold_ref[:, rows] != 0
        member = jnp.where((cohort_ref[:, rows] == cohorts) & train, 1.0, 0.0).astype(jnp.bfloat16)
        present = lax.dot_general(
            member, pres[...].astype(jnp.bfloat16), (((0,), (0,)), ((), ())),
            preferred_element_type=jnp.float32,
        )
        weighted = geno[rows, :] * present.astype(jnp.bfloat16)
        target = 2.0 * pheno_ref[:, rows].astype(jnp.float32) - 1.0
        target = jnp.broadcast_to(target, (16, chunk)).astype(jnp.bfloat16)
        flipped = weighted.T
        start = 0
        for stop in range(TILE, width + 1, TILE):
            left = jnp.concatenate([flipped[:stop], target], axis=0)
            part = jnp.dot(
                left, weighted[:, stop - TILE : stop], preferred_element_type=jnp.float32
            )
            gram[start : start + stop + 8, :] += part[: stop + 8]
            start += stop + 8
        return 0

    lax.fori_loop(0, chunks, body, 0)


def sum_gram(gram, from_core, over_chip, mine_s, smp, sems):
    core_send, core_recv, chip_send, chip_recv, back_send, back_recv = sems
    chips = smp // 2
    core, chip = lax.rem(mine_s, 2), mine_s // 2
    sibling = mine_s + 1 - 2 * core
    half = gram.shape[0] // 2
    size = half // PARTS

    def rows_of(owner, part):
        return pl.ds(pl.multiple_of(owner * half + part * size, 8), size)

    first = []
    for part in range(PARTS):
        copy = pltpu.make_async_remote_copy(
            src_ref=gram.at[rows_of(1 - core, part)],
            dst_ref=from_core.at[part],
            send_sem=core_send.at[part],
            recv_sem=core_recv.at[part],
            device_id={"smp": sibling},
            device_id_type=MESH,
        )
        copy.start()
        first.append(copy)
    second = []
    for part in range(PARTS):
        first[part].wait_recv()
        over_chip[chip, part] = gram[rows_of(core, part), :] + from_core[part]
        row = []
        for distance in range(1, chips):
            peer = lax.rem(chip + distance, chips)
            copy = pltpu.make_async_remote_copy(
                src_ref=over_chip.at[chip, part],
                dst_ref=over_chip.at[chip, part],
                send_sem=chip_send.at[distance, part],
                recv_sem=chip_recv.at[distance, part],
                device_id={"smp": peer * 2 + core},
                device_id_type=MESH,
            )
            copy.start()
            row.append(copy)
        second.append(row)
    return first, second, sibling, rows_of


def finish_gram(full, over_chip, mine_s, smp, sems, first, second, sibling, rows_of):
    back_send, back_recv = sems[4:]
    core = lax.rem(mine_s, 2)
    third = []
    for part in range(PARTS):
        for copy in second[part]:
            copy.wait_recv()
        total = over_chip[0, part]
        for chip in range(1, smp // 2):
            total = total + over_chip[chip, part]
        full[rows_of(core, part), :] = total
        copy = pltpu.make_async_remote_copy(
            src_ref=full.at[rows_of(core, part)],
            dst_ref=full.at[rows_of(core, part)],
            send_sem=back_send.at[part],
            recv_sem=back_recv.at[part],
            device_id={"smp": sibling},
            device_id_type=MESH,
        )
        copy.start()
        third.append(copy)
    for copy in third:
        copy.wait_recv()
    for copy in first + [copy for row in second for copy in row] + third:
        copy.wait_send()


def ridge_solve(full, square, width, total_samples):
    cross = []
    start = 0
    for stop in range(TILE, width + 1, TILE):
        column = slice(stop - TILE, stop)
        for row in range(0, stop, TILE):
            block = full[start + row : start + row + TILE, :]
            for piece in range(3):
                part = block.astype(jnp.bfloat16)
                square[piece, row : row + TILE, column] = part
                block = block - part.astype(jnp.float32)
            if row + TILE < stop:
                block = full[start + row : start + row + TILE, :].T
                for piece in range(3):
                    part = block.astype(jnp.bfloat16)
                    square[piece, column, row : row + TILE] = part
                    block = block - part.astype(jnp.float32)
        cross.append(full[start + stop : start + stop + 1, :])
        start += stop + 8
    rank = lax.broadcasted_iota(jnp.int32, (8, 1), 0)
    shifts = jnp.full((8, 1), penalty_list[-1] * total_samples, jnp.float32)
    for index, penalty in enumerate(penalty_list):
        shifts = jnp.where(rank == index, jnp.float32(penalty * total_samples), shifts)
    residual = jnp.broadcast_to(jnp.concatenate(cross, axis=1), (8, width))
    solution = jnp.zeros_like(residual)
    direction = residual
    norm_now = jnp.sum(residual * residual, axis=1, keepdims=True)
    for ridge_step in range(RIDGE_STEPS):
        middle = low_part(direction)
        stacked = jnp.concatenate([direction, middle, low_part(middle)], axis=0)
        stacked = stacked.astype(jnp.bfloat16)
        product = jnp.dot(stacked, square[0], preferred_element_type=jnp.float32)
        for piece in range(1, 3):
            product = product + jnp.dot(
                stacked, square[piece], preferred_element_type=jnp.float32
            )
        image = product[:8] + (product[8:16] + product[16:24]) + shifts * direction
        alpha = norm_now / jnp.sum(direction * image, axis=1, keepdims=True)
        solution = solution + alpha * direction
        if ridge_step < RIDGE_STEPS - 1:
            residual = residual - alpha * image
            norm_next = jnp.sum(residual * residual, axis=1, keepdims=True)
            direction = residual + (norm_next / norm_now) * direction
            norm_now = norm_next
    return solution.astype(jnp.bfloat16)


def whole_kernel(
    blk, smp, total_samples, cohort_count,
    geno_ref, presence_ref, cohort_ref, fold_ref, pheno_ref, level_ref, linear_ref,
    geno, pres, gram, from_core, over_chip, full, square, masked_ridge, scores_ref,
    gathered, packed, pieces, smp_part, blk_part,
    load_sem, core_send, core_recv, chip_send, chip_recv, back_send, back_recv,
    score_send, score_recv, smp_send, smp_recv, blk_send, blk_recv,
):
    mine_b = lax.axis_index("blk")
    mine_s = lax.axis_index("smp")
    per_block = scores_ref.shape[0]
    owned = packed.shape[1]
    predictors = packed.shape[0]
    local_count, width = geno.shape
    chunks = load_sem.shape[0]
    chunk = local_count // chunks

    def load(index):
        rows = pl.ds(pl.multiple_of(index * chunk, chunk), chunk)
        return pltpu.make_async_copy(geno_ref.at[rows], geno.at[rows], load_sem.at[index])

    for index in range(chunks):
        load(index).start()
    barrier = pltpu.get_barrier_semaphore()
    for distance in range(1, blk):
        pl.semaphore_signal(
            barrier, inc=1, device_id={"blk": lax.rem(mine_b + distance, blk)}, device_id_type=MESH
        )
    for distance in range(1, smp):
        pl.semaphore_signal(
            barrier, inc=1, device_id={"smp": lax.rem(mine_s + distance, smp)}, device_id_type=MESH
        )
    pres[...] = jnp.zeros_like(pres)
    pres[:cohort_count, :] = presence_ref[...].astype(jnp.float32)
    accumulate_gram(chunk, chunks, load, geno, pres, cohort_ref, fold_ref, pheno_ref, gram)
    pl.semaphore_wait(barrier, blk + smp - 2)

    sems = (core_send, core_recv, chip_send, chip_recv, back_send, back_recv)
    state = sum_gram(gram, from_core, over_chip, mine_s, smp, sems)
    finish_gram(full, over_chip, mine_s, smp, sems, *state)
    ridge = ridge_solve(full, square, width, total_samples).astype(jnp.float32)
    for cohort in range(cohort_count):
        masked_ridge[cohort * 8 : cohort * 8 + 8, :] = (
            ridge * pres[cohort : cohort + 1, :]
        ).astype(jnp.bfloat16)
    scale = jnp.sqrt(jnp.float32(total_samples) / width)

    def score_copy(distance):
        target = lax.rem(mine_b + distance, blk)
        return pltpu.make_async_remote_copy(
            src_ref=scores_ref.at[:, pl.ds(pl.multiple_of(target * owned, LANES), owned)],
            dst_ref=gathered.at[mine_b],
            send_sem=score_send.at[distance],
            recv_sem=score_recv.at[distance],
            device_id={"blk": target},
            device_id_type=MESH,
        )

    def score_chunk(distance):
        target = lax.rem(mine_b + distance, blk)
        rows = pl.ds(pl.multiple_of(target * owned, LANES), owned)
        each = lax.dot_general(
            masked_ridge[...], geno[rows, :], (((1,), (1,)), ((), ())),
            preferred_element_type=jnp.float32,
        )
        cohort = cohort_ref[:, rows]
        chosen = each[:8]
        for index in range(1, cohort_count):
            chosen = jnp.where(cohort == index, each[index * 8 : index * 8 + 8], chosen)
        scores_ref[:, rows] = chosen[:per_block] * scale

    def score_step(distance, _):
        score_chunk(distance)
        score_copy(distance).start()
        return 0

    lax.fori_loop(1, blk, score_step, 0)
    score_chunk(0)
    copies = [score_copy(distance) for distance in range(1, blk)]
    own = pl.ds(pl.multiple_of(mine_b * owned, LANES), owned)
    gathered[mine_b] = scores_ref[:, own]
    labels = pheno_ref[:, own].astype(jnp.float32)
    train = (fold_ref[:, own] != 0).astype(jnp.float32)
    for copy in copies:
        copy.wait_recv()
    for block in range(blk):
        packed[block * per_block : (block + 1) * per_block, :] = gathered[block]
    scores = packed[...]
    pieces[...] = jnp.concatenate([scores, low_part(scores)], axis=0).astype(jnp.bfloat16)
    for copy in copies:
        copy.wait_send()

    width = predictors + 8
    pad_row = lax.broadcasted_iota(jnp.int32, (8, owned), 0)
    row_of = lax.broadcasted_iota(jnp.int32, (predictors, width), 0)
    column_of = lax.broadcasted_iota(jnp.int32, (predictors, width), 1)
    ridge = level_ridge * total_samples

    def predict(level):
        return jnp.sum(
            packed[...] * jnp.concatenate([level] * (owned // LANES), axis=1), axis=0, keepdims=True
        )

    def widen(level):
        return jnp.concatenate([level] * pl.cdiv(width, LANES), axis=1)[:, :width]

    def newton(step, level):
        prob = jax.nn.sigmoid(predict(level))
        resid = train * (labels - prob)
        curve = train * prob * (1.0 - prob)
        right = jnp.concatenate(
            [packed[...] * curve, jnp.where(pad_row == 0, resid, 0.0)], axis=0
        )
        moments = jnp.zeros((2 * predictors, width), jnp.float32)
        for part in (right, low_part(right)):
            moments = moments + lax.dot_general(
                pieces[...], part.astype(jnp.bfloat16), (((1,), (1,)), ((), ())),
                preferred_element_type=jnp.float32,
            )
        smp_part[step, mine_s] = moments[:predictors] + moments[predictors:]
        over_smp = exchange(
            smp_part.at[step], mine_s, "smp", smp, smp_send.at[step], smp_recv.at[step]
        )
        blk_part[step, mine_b] = over_smp
        system = exchange(
            blk_part.at[step], mine_b, "blk", blk, blk_send.at[step], blk_recv.at[step]
        )
        system = jnp.where(row_of == column_of, system + ridge, system)
        system = jnp.where(column_of == predictors, system - ridge * widen(level), system)
        return level + spd_solve(system, predictors)

    level = lax.fori_loop(0, NEWTON, newton, jnp.zeros((predictors, LANES), jnp.float32))
    linear_ref[...] = predict(level)
    diagonal = row_of == column_of
    level_ref[...] = jnp.sum(jnp.where(diagonal, widen(level), 0.0), axis=0, keepdims=True)[
        :, :predictors
    ]


def on_device(genotype, presence, cohort_id, fold_id, phenotype):
    blk = lax.axis_size("blk")
    smp = lax.axis_size("smp")
    local_count, block_width = genotype.shape
    total_samples = local_count * smp
    per_block = len(penalty_list)
    owned = local_count // blk
    predictors = per_block * blk
    width = predictors + 8
    cohort_count = presence.shape[0]
    half = gram_rows(block_width) // 2
    size = half // PARTS
    chips = smp // 2
    dma = pltpu.SemaphoreType.DMA
    vmem = pl.BlockSpec(memory_space=pltpu.VMEM)
    level, linear = pl.pallas_call(
        functools.partial(whole_kernel, blk, smp, total_samples, cohort_count),
        out_shape=(
            jax.ShapeDtypeStruct((1, predictors), jnp.float32),
            jax.ShapeDtypeStruct((1, owned), jnp.float32),
        ),
        in_specs=[pl.BlockSpec(memory_space=pl.ANY)] + [vmem] * 4,
        out_specs=(vmem,) * 2,
        scratch_shapes=[
            pltpu.VMEM((local_count, block_width), jnp.bfloat16),
            pltpu.VMEM((8, block_width), jnp.float32),
            pltpu.VMEM((2 * half, TILE), jnp.float32),
            pltpu.VMEM((PARTS, size, TILE), jnp.float32),
            pltpu.VMEM((chips, PARTS, size, TILE), jnp.float32),
            pltpu.VMEM((2 * half, TILE), jnp.float32),
            pltpu.VMEM((3, block_width, block_width), jnp.bfloat16),
            pltpu.VMEM((8 * cohort_count, block_width), jnp.bfloat16),
            pltpu.VMEM((per_block, local_count), jnp.float32),
            pltpu.VMEM((blk, per_block, owned), jnp.float32),
            pltpu.VMEM((predictors, owned), jnp.float32),
            pltpu.VMEM((2 * predictors, owned), jnp.bfloat16),
            pltpu.VMEM((NEWTON, smp, predictors, width), jnp.float32),
            pltpu.VMEM((NEWTON, blk, predictors, width), jnp.float32),
            dma((local_count // CHUNK,)),
            dma((PARTS,)), dma((PARTS,)),
            dma((chips, PARTS)), dma((chips, PARTS)),
            dma((PARTS,)), dma((PARTS,)),
            dma((blk,)), dma((blk,)),
            dma((NEWTON, smp)), dma((NEWTON, smp)),
            dma((NEWTON, blk)), dma((NEWTON, blk)),
        ],
        compiler_params=pltpu.CompilerParams(
            collective_id=0, has_side_effects=True, vmem_limit_bytes=56 * 1024 * 1024
        ),
    )(
        genotype, presence, cohort_id.reshape(1, -1), fold_id.reshape(1, -1),
        phenotype.reshape(1, -1),
    )
    return level.reshape(predictors), linear.reshape(owned)


def solution(mesh):
    in_specs = (P("smp", "blk"), P(None, "blk"), P("smp"), P("smp"), P("smp"))
    out_specs = (P(), P(("smp", "blk")))
    return jax.shard_map(
        on_device, mesh=mesh, in_specs=in_specs, out_specs=out_specs, check_vma=False
    )
```

```python
import functools

import jax
import jax.numpy as jnp
from jax import lax
from jax.experimental import pallas as pl
from jax.experimental.pallas import tpu as pltpu
from jax.sharding import PartitionSpec as P

NEWTON = 4
RIDGE_STEPS = 6
PANEL = 8
LANES = 128
TILE = 256
PARTS = 7
CHUNK = 2048
MESH = pl.DeviceIdType.MESH


penalty_list = (0.002, 0.01, 0.05, 0.25, 1.25)
level_ridge = 0.05


def low_part(value):
    return value - value.astype(jnp.bfloat16).astype(jnp.float32)


def spd_solve(system, order):
    width = system.shape[1]
    row_of = lax.broadcasted_iota(jnp.int32, (order, width), 0)
    row_of_lane = lax.broadcasted_iota(jnp.int32, (order, LANES), 0)
    for start in range(0, order, PANEL):
        stop = min(start + PANEL, order)
        columns = [
            jnp.broadcast_to(system[:, j : j + 1], (order, LANES)) for j in range(start, stop)
        ]
        for j in range(start, stop):
            column = columns[j - start]
            inverse = 1.0 / column[j : j + 1, :]
            pivot_row = system[j : j + 1, :] * jnp.concatenate(
                [inverse] * pl.cdiv(width, LANES), axis=1
            )[:, :width]
            wide = jnp.concatenate([column] * pl.cdiv(width, LANES), axis=1)[:, :width]
            system = jnp.where(row_of == j, pivot_row, system - wide * pivot_row)
            for k in range(j + 1, stop):
                other = columns[k - start]
                entry = other[j : j + 1, :] * inverse
                columns[k - start] = jnp.where(row_of_lane == j, entry, other - column * entry)
    return jnp.broadcast_to(system[:, order : order + 1], (order, LANES))


def pack_plan(predictors):
    lanes = -(-(predictors + 1) // 2) * 2
    groups = max(1, LANES // lanes)
    rows = -(-predictors // (8 * groups)) * 8
    return lanes, groups, rows, -(-lanes * groups // LANES) * LANES


def pack_rows(system):
    lanes, groups, rows, width = pack_plan(system.shape[0])
    out = system[:rows]
    for group in range(1, groups):
        block = system[group * rows : (group + 1) * rows]
        if block.shape[0] < rows:
            block = jnp.concatenate(
                [block, jnp.zeros((rows - block.shape[0], width), jnp.float32)], axis=0
            )
        out = out + pltpu.roll(block, group * lanes, 1)
    return out


def unpack_rows(packed_rows, predictors):
    lanes, groups, rows, width = pack_plan(predictors)
    blocks = [packed_rows]
    for group in range(1, groups):
        block = pltpu.roll(packed_rows, width - group * lanes, 1)
        blocks.append(block[: min(rows, predictors - group * rows)])
    return jnp.concatenate(blocks, axis=0)


def exchange(ref, mine, axis, count, send_sem, recv_sem):
    copies = []
    for distance in range(1, count):
        copy = pltpu.make_async_remote_copy(
            src_ref=ref.at[mine],
            dst_ref=ref.at[mine],
            send_sem=send_sem.at[distance],
            recv_sem=recv_sem.at[distance],
            device_id={axis: lax.rem(mine + distance, count)},
            device_id_type=MESH,
        )
        copy.start()
        copies.append(copy)
    for copy in copies:
        copy.wait_recv()
    total = ref[0]
    for slot in range(1, count):
        total = total + ref[slot]
    for copy in copies:
        copy.wait_send()
    return total


def gram_rows(width):
    return sum(stop + 8 for stop in range(TILE, width + 1, TILE))


def accumulate_gram(chunk, chunks, load, geno, pres, cohort_ref, fold_ref, pheno_ref, gram):
    width = geno.shape[1]
    cohorts = lax.broadcasted_iota(jnp.int32, (pres.shape[0], chunk), 0)
    gram[...] = jnp.zeros_like(gram)

    def body(index, _):
        load(index).wait()
        rows = pl.ds(pl.multiple_of(index * chunk, chunk), chunk)
        train = fold_ref[:, rows] != 0
        member = jnp.where((cohort_ref[:, rows] == cohorts) & train, 1.0, 0.0).astype(jnp.bfloat16)
        present = lax.dot_general(
            member, pres[...].astype(jnp.bfloat16), (((0,), (0,)), ((), ())),
            preferred_element_type=jnp.float32,
        )
        weighted = geno[rows, :] * present.astype(jnp.bfloat16)
        target = 2.0 * pheno_ref[:, rows].astype(jnp.float32) - 1.0
        target = jnp.broadcast_to(target, (16, chunk)).astype(jnp.bfloat16)
        flipped = weighted.T
        start = 0
        for stop in range(TILE, width + 1, TILE):
            left = jnp.concatenate([flipped[:stop], target], axis=0)
            part = jnp.dot(
                left, weighted[:, stop - TILE : stop], preferred_element_type=jnp.float32
            )
            gram[start : start + stop + 8, :] += part[: stop + 8]
            start += stop + 8
        return 0

    lax.fori_loop(0, chunks, body, 0)


def sum_gram(gram, from_core, over_chip, mine_s, smp, sems):
    core_send, core_recv, chip_send, chip_recv, back_send, back_recv = sems
    chips = smp // 2
    core, chip = lax.rem(mine_s, 2), mine_s // 2
    sibling = mine_s + 1 - 2 * core
    half = gram.shape[0] // 2
    size = half // PARTS

    def rows_of(owner, part):
        return pl.ds(pl.multiple_of(owner * half + part * size, 8), size)

    first = []
    for part in range(PARTS):
        copy = pltpu.make_async_remote_copy(
            src_ref=gram.at[rows_of(1 - core, part)],
            dst_ref=from_core.at[part],
            send_sem=core_send.at[part],
            recv_sem=core_recv.at[part],
            device_id={"smp": sibling},
            device_id_type=MESH,
        )
        copy.start()
        first.append(copy)
    second = []
    for part in range(PARTS):
        first[part].wait_recv()
        over_chip[chip, part] = gram[rows_of(core, part), :] + from_core[part]
        row = []
        for distance in range(1, chips):
            peer = lax.rem(chip + distance, chips)
            copy = pltpu.make_async_remote_copy(
                src_ref=over_chip.at[chip, part],
                dst_ref=over_chip.at[chip, part],
                send_sem=chip_send.at[distance, part],
                recv_sem=chip_recv.at[distance, part],
                device_id={"smp": peer * 2 + core},
                device_id_type=MESH,
            )
            copy.start()
            row.append(copy)
        second.append(row)
    return first, second, sibling, rows_of


def finish_gram(full, over_chip, mine_s, smp, sems, first, second, sibling, rows_of):
    back_send, back_recv = sems[4:]
    core = lax.rem(mine_s, 2)
    third = []
    for part in range(PARTS):
        for copy in second[part]:
            copy.wait_recv()
        total = over_chip[0, part]
        for chip in range(1, smp // 2):
            total = total + over_chip[chip, part]
        full[rows_of(core, part), :] = total
        copy = pltpu.make_async_remote_copy(
            src_ref=full.at[rows_of(core, part)],
            dst_ref=full.at[rows_of(core, part)],
            send_sem=back_send.at[part],
            recv_sem=back_recv.at[part],
            device_id={"smp": sibling},
            device_id_type=MESH,
        )
        copy.start()
        third.append(copy)
    for copy in third:
        copy.wait_recv()
    for copy in first + [copy for row in second for copy in row] + third:
        copy.wait_send()


def ridge_solve(full, square, width, total_samples):
    cross = []
    start = 0
    for stop in range(TILE, width + 1, TILE):
        column = slice(stop - TILE, stop)
        for row in range(0, stop, TILE):
            block = full[start + row : start + row + TILE, :]
            for piece in range(3):
                part = block.astype(jnp.bfloat16)
                square[piece, row : row + TILE, column] = part
                block = block - part.astype(jnp.float32)
            if row + TILE < stop:
                block = full[start + row : start + row + TILE, :].T
                for piece in range(3):
                    part = block.astype(jnp.bfloat16)
                    square[piece, column, row : row + TILE] = part
                    block = block - part.astype(jnp.float32)
        cross.append(full[start + stop : start + stop + 1, :])
        start += stop + 8
    rank = lax.broadcasted_iota(jnp.int32, (8, 1), 0)
    shifts = jnp.full((8, 1), penalty_list[-1] * total_samples, jnp.float32)
    for index, penalty in enumerate(penalty_list):
        shifts = jnp.where(rank == index, jnp.float32(penalty * total_samples), shifts)
    residual = jnp.broadcast_to(jnp.concatenate(cross, axis=1), (8, width))
    solution = jnp.zeros_like(residual)
    direction = residual
    norm_now = jnp.sum(residual * residual, axis=1, keepdims=True)
    for ridge_step in range(RIDGE_STEPS):
        middle = low_part(direction)
        stacked = jnp.concatenate([direction, middle, low_part(middle)], axis=0)
        stacked = stacked.astype(jnp.bfloat16)
        product = jnp.dot(stacked, square[0], preferred_element_type=jnp.float32)
        for piece in range(1, 3):
            product = product + jnp.dot(
                stacked, square[piece], preferred_element_type=jnp.float32
            )
        image = product[:8] + (product[8:16] + product[16:24]) + shifts * direction
        alpha = norm_now / jnp.sum(direction * image, axis=1, keepdims=True)
        solution = solution + alpha * direction
        if ridge_step < RIDGE_STEPS - 1:
            residual = residual - alpha * image
            norm_next = jnp.sum(residual * residual, axis=1, keepdims=True)
            direction = residual + (norm_next / norm_now) * direction
            norm_now = norm_next
    return solution.astype(jnp.bfloat16)


def whole_kernel(
    blk, smp, total_samples, cohort_count,
    geno_ref, presence_ref, cohort_ref, fold_ref, pheno_ref, level_ref, linear_ref,
    geno, pres, gram, from_core, over_chip, full, square, masked_ridge, scores_ref,
    gathered, packed, pieces, smp_part, blk_part,
    load_sem, core_send, core_recv, chip_send, chip_recv, back_send, back_recv,
    score_send, score_recv, smp_send, smp_recv, blk_send, blk_recv,
):
    mine_b = lax.axis_index("blk")
    mine_s = lax.axis_index("smp")
    per_block = scores_ref.shape[0]
    owned = packed.shape[1]
    predictors = packed.shape[0]
    local_count, width = geno.shape
    chunks = load_sem.shape[0]
    chunk = local_count // chunks

    def load(index):
        rows = pl.ds(pl.multiple_of(index * chunk, chunk), chunk)
        return pltpu.make_async_copy(geno_ref.at[rows], geno.at[rows], load_sem.at[index])

    for index in range(chunks):
        load(index).start()
    barrier = pltpu.get_barrier_semaphore()
    for distance in range(1, blk):
        pl.semaphore_signal(
            barrier, inc=1, device_id={"blk": lax.rem(mine_b + distance, blk)}, device_id_type=MESH
        )
    for distance in range(1, smp):
        pl.semaphore_signal(
            barrier, inc=1, device_id={"smp": lax.rem(mine_s + distance, smp)}, device_id_type=MESH
        )
    pres[...] = jnp.zeros_like(pres)
    pres[:cohort_count, :] = presence_ref[...].astype(jnp.float32)
    accumulate_gram(chunk, chunks, load, geno, pres, cohort_ref, fold_ref, pheno_ref, gram)
    pl.semaphore_wait(barrier, blk + smp - 2)

    sems = (core_send, core_recv, chip_send, chip_recv, back_send, back_recv)
    state = sum_gram(gram, from_core, over_chip, mine_s, smp, sems)
    finish_gram(full, over_chip, mine_s, smp, sems, *state)
    ridge = ridge_solve(full, square, width, total_samples).astype(jnp.float32)
    for cohort in range(cohort_count):
        masked_ridge[cohort * 8 : cohort * 8 + 8, :] = (
            ridge * pres[cohort : cohort + 1, :]
        ).astype(jnp.bfloat16)
    scale = jnp.sqrt(jnp.float32(total_samples) / width)

    def score_copy(distance):
        target = lax.rem(mine_b + distance, blk)
        return pltpu.make_async_remote_copy(
            src_ref=scores_ref.at[:, pl.ds(pl.multiple_of(target * owned, LANES), owned)],
            dst_ref=gathered.at[mine_b],
            send_sem=score_send.at[distance],
            recv_sem=score_recv.at[distance],
            device_id={"blk": target},
            device_id_type=MESH,
        )

    def score_chunk(distance):
        target = lax.rem(mine_b + distance, blk)
        rows = pl.ds(pl.multiple_of(target * owned, LANES), owned)
        each = lax.dot_general(
            masked_ridge[...], geno[rows, :], (((1,), (1,)), ((), ())),
            preferred_element_type=jnp.float32,
        )
        cohort = cohort_ref[:, rows]
        chosen = each[:8]
        for index in range(1, cohort_count):
            chosen = jnp.where(cohort == index, each[index * 8 : index * 8 + 8], chosen)
        scores_ref[:, rows] = chosen[:per_block] * scale

    def score_step(distance, _):
        score_chunk(distance)
        score_copy(distance).start()
        return 0

    lax.fori_loop(1, blk, score_step, 0)
    score_chunk(0)
    copies = [score_copy(distance) for distance in range(1, blk)]
    own = pl.ds(pl.multiple_of(mine_b * owned, LANES), owned)
    gathered[mine_b] = scores_ref[:, own]
    labels = pheno_ref[:, own].astype(jnp.float32)
    train = (fold_ref[:, own] != 0).astype(jnp.float32)
    for copy in copies:
        copy.wait_recv()
    for block in range(blk):
        packed[block * per_block : (block + 1) * per_block, :] = gathered[block]
    scores = packed[...]
    pieces[...] = jnp.concatenate([scores, low_part(scores)], axis=0).astype(jnp.bfloat16)
    for copy in copies:
        copy.wait_send()

    width = pack_plan(predictors)[3]
    pad_row = lax.broadcasted_iota(jnp.int32, (width - predictors, owned), 0)
    row_of = lax.broadcasted_iota(jnp.int32, (predictors, width), 0)
    column_of = lax.broadcasted_iota(jnp.int32, (predictors, width), 1)
    ridge = level_ridge * total_samples

    def predict(level):
        return jnp.sum(
            packed[...] * jnp.concatenate([level] * (owned // LANES), axis=1), axis=0, keepdims=True
        )

    def widen(level):
        return jnp.concatenate([level] * pl.cdiv(width, LANES), axis=1)[:, :width]

    def newton(step, level):
        prob = jax.nn.sigmoid(predict(level))
        resid = train * (labels - prob)
        curve = train * prob * (1.0 - prob)
        right = jnp.concatenate(
            [packed[...] * curve, jnp.where(pad_row == 0, resid, 0.0)], axis=0
        )
        moments = jnp.zeros((2 * predictors, width), jnp.float32)
        for part in (right, low_part(right)):
            moments = moments + lax.dot_general(
                pieces[...], part.astype(jnp.bfloat16), (((1,), (1,)), ((), ())),
                preferred_element_type=jnp.float32,
            )
        smp_part[step, mine_s] = pack_rows(moments[:predictors] + moments[predictors:])
        over_smp = exchange(
            smp_part.at[step], mine_s, "smp", smp, smp_send.at[step], smp_recv.at[step]
        )
        blk_part[step, mine_b] = over_smp
        system = exchange(
            blk_part.at[step], mine_b, "blk", blk, blk_send.at[step], blk_recv.at[step]
        )
        system = unpack_rows(system, predictors)
        system = jnp.where(row_of == column_of, system + ridge, system)
        system = jnp.where(column_of == predictors, system - ridge * widen(level), system)
        return level + spd_solve(system, predictors)

    level = lax.fori_loop(0, NEWTON, newton, jnp.zeros((predictors, LANES), jnp.float32))
    linear_ref[...] = predict(level)
    diagonal = row_of == column_of
    level_ref[...] = jnp.sum(jnp.where(diagonal, widen(level), 0.0), axis=0, keepdims=True)[
        :, :predictors
    ]


def on_device(genotype, presence, cohort_id, fold_id, phenotype):
    blk = lax.axis_size("blk")
    smp = lax.axis_size("smp")
    local_count, block_width = genotype.shape
    total_samples = local_count * smp
    per_block = len(penalty_list)
    owned = local_count // blk
    predictors = per_block * blk
    system_rows, system_lanes = pack_plan(predictors)[2:]
    cohort_count = presence.shape[0]
    half = gram_rows(block_width) // 2
    size = half // PARTS
    chips = smp // 2
    dma = pltpu.SemaphoreType.DMA
    vmem = pl.BlockSpec(memory_space=pltpu.VMEM)
    level, linear = pl.pallas_call(
        functools.partial(whole_kernel, blk, smp, total_samples, cohort_count),
        out_shape=(
            jax.ShapeDtypeStruct((1, predictors), jnp.float32),
            jax.ShapeDtypeStruct((1, owned), jnp.float32),
        ),
        in_specs=[pl.BlockSpec(memory_space=pl.ANY)] + [vmem] * 4,
        out_specs=(vmem,) * 2,
        scratch_shapes=[
            pltpu.VMEM((local_count, block_width), jnp.bfloat16),
            pltpu.VMEM((8, block_width), jnp.float32),
            pltpu.VMEM((2 * half, TILE), jnp.float32),
            pltpu.VMEM((PARTS, size, TILE), jnp.float32),
            pltpu.VMEM((chips, PARTS, size, TILE), jnp.float32),
            pltpu.VMEM((2 * half, TILE), jnp.float32),
            pltpu.VMEM((3, block_width, block_width), jnp.bfloat16),
            pltpu.VMEM((8 * cohort_count, block_width), jnp.bfloat16),
            pltpu.VMEM((per_block, local_count), jnp.float32),
            pltpu.VMEM((blk, per_block, owned), jnp.float32),
            pltpu.VMEM((predictors, owned), jnp.float32),
            pltpu.VMEM((2 * predictors, owned), jnp.bfloat16),
            pltpu.VMEM((NEWTON, smp, system_rows, system_lanes), jnp.float32),
            pltpu.VMEM((NEWTON, blk, system_rows, system_lanes), jnp.float32),
            dma((local_count // CHUNK,)),
            dma((PARTS,)), dma((PARTS,)),
            dma((chips, PARTS)), dma((chips, PARTS)),
            dma((PARTS,)), dma((PARTS,)),
            dma((blk,)), dma((blk,)),
            dma((NEWTON, smp)), dma((NEWTON, smp)),
            dma((NEWTON, blk)), dma((NEWTON, blk)),
        ],
        compiler_params=pltpu.CompilerParams(
            collective_id=0, has_side_effects=True, vmem_limit_bytes=56 * 1024 * 1024
        ),
    )(
        genotype, presence, cohort_id.reshape(1, -1), fold_id.reshape(1, -1),
        phenotype.reshape(1, -1),
    )
    return level.reshape(predictors), linear.reshape(owned)


def solution(mesh):
    in_specs = (P("smp", "blk"), P(None, "blk"), P("smp"), P("smp"), P("smp"))
    out_specs = (P(), P(("smp", "blk")))
    return jax.shard_map(
        on_device, mesh=mesh, in_specs=in_specs, out_specs=out_specs, check_vma=False
    )
```

```python
import functools

import jax
import jax.numpy as jnp
from jax import lax
from jax.experimental import pallas as pl
from jax.experimental.pallas import tpu as pltpu
from jax.sharding import PartitionSpec as P

NEWTON = 4
RIDGE_STEPS = 6
PANEL = 8
LANES = 128
TILE = 256
PARTS = 7
CHUNK = 2048
MESH = pl.DeviceIdType.MESH


penalty_list = (0.002, 0.01, 0.05, 0.25, 1.25)
level_ridge = 0.05


def low_part(value):
    return value - value.astype(jnp.bfloat16).astype(jnp.float32)


def spd_solve(system, order):
    width = system.shape[1]
    row_of = lax.broadcasted_iota(jnp.int32, (order, width), 0)
    row_of_lane = lax.broadcasted_iota(jnp.int32, (order, LANES), 0)
    for start in range(0, order, PANEL):
        stop = min(start + PANEL, order)
        columns = [
            jnp.broadcast_to(system[:, j : j + 1], (order, LANES)) for j in range(start, stop)
        ]
        for j in range(start, stop):
            column = columns[j - start]
            inverse = 1.0 / column[j : j + 1, :]
            pivot_row = system[j : j + 1, :] * jnp.concatenate(
                [inverse] * pl.cdiv(width, LANES), axis=1
            )[:, :width]
            wide = jnp.concatenate([column] * pl.cdiv(width, LANES), axis=1)[:, :width]
            system = jnp.where(row_of == j, pivot_row, system - wide * pivot_row)
            for k in range(j + 1, stop):
                other = columns[k - start]
                entry = other[j : j + 1, :] * inverse
                columns[k - start] = jnp.where(row_of_lane == j, entry, other - column * entry)
    return jnp.broadcast_to(system[:, order : order + 1], (order, LANES))


def pack_plan(predictors):
    lanes = -(-(predictors + 1) // 2) * 2
    groups = max(1, LANES // lanes)
    rows = -(-predictors // (8 * groups)) * 8
    return lanes, groups, rows, -(-lanes * groups // LANES) * LANES


def pack_rows(system):
    lanes, groups, rows, width = pack_plan(system.shape[0])
    out = system[:rows]
    for group in range(1, groups):
        block = system[group * rows : (group + 1) * rows]
        if block.shape[0] < rows:
            block = jnp.concatenate(
                [block, jnp.zeros((rows - block.shape[0], width), jnp.float32)], axis=0
            )
        out = out + pltpu.roll(block, group * lanes, 1)
    return out


def unpack_rows(packed_rows, predictors):
    lanes, groups, rows, width = pack_plan(predictors)
    blocks = [packed_rows]
    for group in range(1, groups):
        block = pltpu.roll(packed_rows, width - group * lanes, 1)
        blocks.append(block[: min(rows, predictors - group * rows)])
    return jnp.concatenate(blocks, axis=0)


def exchange(ref, mine, axis, count, send_sem, recv_sem):
    copies = []
    for distance in range(1, count):
        copy = pltpu.make_async_remote_copy(
            src_ref=ref.at[mine],
            dst_ref=ref.at[mine],
            send_sem=send_sem.at[distance],
            recv_sem=recv_sem.at[distance],
            device_id={axis: lax.rem(mine + distance, count)},
            device_id_type=MESH,
        )
        copy.start()
        copies.append(copy)
    for copy in copies:
        copy.wait_recv()
    total = ref[0]
    for slot in range(1, count):
        total = total + ref[slot]
    for copy in copies:
        copy.wait_send()
    return total


def gram_rows(width):
    return sum(stop + 8 for stop in range(TILE, width + 1, TILE))


def accumulate_gram(chunk, chunks, load, geno, pres, cohort_ref, fold_ref, pheno_ref, gram):
    width = geno.shape[1]
    cohorts = lax.broadcasted_iota(jnp.int32, (pres.shape[0], chunk), 0)
    gram[...] = jnp.zeros_like(gram)

    def body(index, _):
        load(index).wait()
        rows = pl.ds(pl.multiple_of(index * chunk, chunk), chunk)
        train = fold_ref[:, rows] != 0
        member = jnp.where((cohort_ref[:, rows] == cohorts) & train, 1.0, 0.0).astype(jnp.bfloat16)
        present = lax.dot_general(
            member, pres[...].astype(jnp.bfloat16), (((0,), (0,)), ((), ())),
            preferred_element_type=jnp.float32,
        )
        weighted = geno[rows, :] * present.astype(jnp.bfloat16)
        target = 2.0 * pheno_ref[:, rows].astype(jnp.float32) - 1.0
        target = jnp.broadcast_to(target, (16, chunk)).astype(jnp.bfloat16)
        flipped = weighted.T
        start = 0
        for stop in range(TILE, width + 1, TILE):
            left = jnp.concatenate([flipped[:stop], target], axis=0)
            part = jnp.dot(
                left, weighted[:, stop - TILE : stop], preferred_element_type=jnp.float32
            )
            gram[start : start + stop + 8, :] += part[: stop + 8]
            start += stop + 8
        return 0

    lax.fori_loop(0, chunks, body, 0)


def sum_gram(gram, from_core, over_chip, mine_s, smp, sems):
    core_send, core_recv, chip_send, chip_recv, back_send, back_recv = sems
    chips = smp // 2
    core, chip = lax.rem(mine_s, 2), mine_s // 2
    sibling = mine_s + 1 - 2 * core
    half = gram.shape[0] // 2
    size = half // PARTS

    def rows_of(owner, part):
        return pl.ds(pl.multiple_of(owner * half + part * size, 8), size)

    first = []
    for part in range(PARTS):
        copy = pltpu.make_async_remote_copy(
            src_ref=gram.at[rows_of(1 - core, part)],
            dst_ref=from_core.at[part],
            send_sem=core_send.at[part],
            recv_sem=core_recv.at[part],
            device_id={"smp": sibling},
            device_id_type=MESH,
        )
        copy.start()
        first.append(copy)
    second = []
    for part in range(PARTS):
        first[part].wait_recv()
        over_chip[chip, part] = gram[rows_of(core, part), :] + from_core[part]
        row = []
        for distance in range(1, chips):
            peer = lax.rem(chip + distance, chips)
            copy = pltpu.make_async_remote_copy(
                src_ref=over_chip.at[chip, part],
                dst_ref=over_chip.at[chip, part],
                send_sem=chip_send.at[distance, part],
                recv_sem=chip_recv.at[distance, part],
                device_id={"smp": peer * 2 + core},
                device_id_type=MESH,
            )
            copy.start()
            row.append(copy)
        second.append(row)
    return first, second, sibling, rows_of


def finish_gram(full, over_chip, mine_s, smp, sems, first, second, sibling, rows_of):
    back_send, back_recv = sems[4:]
    core = lax.rem(mine_s, 2)
    third = []
    for part in range(PARTS):
        for copy in second[part]:
            copy.wait_recv()
        total = over_chip[0, part]
        for chip in range(1, smp // 2):
            total = total + over_chip[chip, part]
        full[rows_of(core, part), :] = total
        copy = pltpu.make_async_remote_copy(
            src_ref=full.at[rows_of(core, part)],
            dst_ref=full.at[rows_of(core, part)],
            send_sem=back_send.at[part],
            recv_sem=back_recv.at[part],
            device_id={"smp": sibling},
            device_id_type=MESH,
        )
        copy.start()
        third.append(copy)
    for copy in third:
        copy.wait_recv()
    for copy in first + [copy for row in second for copy in row] + third:
        copy.wait_send()


def ridge_solve(full, square, width, total_samples):
    cross = []
    start = 0
    for stop in range(TILE, width + 1, TILE):
        column = slice(stop - TILE, stop)
        for row in range(0, stop, TILE):
            block = full[start + row : start + row + TILE, :]
            for piece in range(2):
                part = block.astype(jnp.bfloat16)
                square[piece, row : row + TILE, column] = part
                block = block - part.astype(jnp.float32)
            if row + TILE < stop:
                block = full[start + row : start + row + TILE, :].T
                for piece in range(2):
                    part = block.astype(jnp.bfloat16)
                    square[piece, column, row : row + TILE] = part
                    block = block - part.astype(jnp.float32)
        cross.append(full[start + stop : start + stop + 1, :])
        start += stop + 8
    rank = lax.broadcasted_iota(jnp.int32, (8, 1), 0)
    shifts = jnp.full((8, 1), penalty_list[-1] * total_samples, jnp.float32)
    for index, penalty in enumerate(penalty_list):
        shifts = jnp.where(rank == index, jnp.float32(penalty * total_samples), shifts)
    residual = jnp.broadcast_to(jnp.concatenate(cross, axis=1), (8, width))
    solution = jnp.zeros_like(residual)
    direction = residual
    norm_now = jnp.sum(residual * residual, axis=1, keepdims=True)
    for ridge_step in range(RIDGE_STEPS):
        middle = low_part(direction)
        stacked = jnp.concatenate([direction, middle, low_part(middle)], axis=0)
        stacked = stacked.astype(jnp.bfloat16)
        product = jnp.dot(stacked, square[0], preferred_element_type=jnp.float32)
        for piece in range(1, 2):
            product = product + jnp.dot(
                stacked, square[piece], preferred_element_type=jnp.float32
            )
        image = product[:8] + (product[8:16] + product[16:24]) + shifts * direction
        alpha = norm_now / jnp.sum(direction * image, axis=1, keepdims=True)
        solution = solution + alpha * direction
        if ridge_step < RIDGE_STEPS - 1:
            residual = residual - alpha * image
            norm_next = jnp.sum(residual * residual, axis=1, keepdims=True)
            direction = residual + (norm_next / norm_now) * direction
            norm_now = norm_next
    return solution.astype(jnp.bfloat16)


def whole_kernel(
    blk, smp, total_samples, cohort_count,
    geno_ref, presence_ref, cohort_ref, fold_ref, pheno_ref, level_ref, linear_ref,
    geno, pres, gram, from_core, over_chip, full, square, masked_ridge, scores_ref,
    gathered, packed, pieces, smp_part, blk_part,
    load_sem, core_send, core_recv, chip_send, chip_recv, back_send, back_recv,
    score_send, score_recv, smp_send, smp_recv, blk_send, blk_recv,
):
    mine_b = lax.axis_index("blk")
    mine_s = lax.axis_index("smp")
    per_block = scores_ref.shape[0]
    owned = packed.shape[1]
    predictors = packed.shape[0]
    local_count, width = geno.shape
    chunks = load_sem.shape[0]
    chunk = local_count // chunks

    def load(index):
        rows = pl.ds(pl.multiple_of(index * chunk, chunk), chunk)
        return pltpu.make_async_copy(geno_ref.at[rows], geno.at[rows], load_sem.at[index])

    for index in range(chunks):
        load(index).start()
    barrier = pltpu.get_barrier_semaphore()
    for distance in range(1, blk):
        pl.semaphore_signal(
            barrier, inc=1, device_id={"blk": lax.rem(mine_b + distance, blk)}, device_id_type=MESH
        )
    for distance in range(1, smp):
        pl.semaphore_signal(
            barrier, inc=1, device_id={"smp": lax.rem(mine_s + distance, smp)}, device_id_type=MESH
        )
    pres[...] = jnp.zeros_like(pres)
    pres[:cohort_count, :] = presence_ref[...].astype(jnp.float32)
    accumulate_gram(chunk, chunks, load, geno, pres, cohort_ref, fold_ref, pheno_ref, gram)
    pl.semaphore_wait(barrier, blk + smp - 2)

    sems = (core_send, core_recv, chip_send, chip_recv, back_send, back_recv)
    state = sum_gram(gram, from_core, over_chip, mine_s, smp, sems)
    finish_gram(full, over_chip, mine_s, smp, sems, *state)
    ridge = ridge_solve(full, square, width, total_samples).astype(jnp.float32)
    for cohort in range(cohort_count):
        masked_ridge[cohort * 8 : cohort * 8 + 8, :] = (
            ridge * pres[cohort : cohort + 1, :]
        ).astype(jnp.bfloat16)
    scale = jnp.sqrt(jnp.float32(total_samples) / width)

    def score_copy(distance):
        target = lax.rem(mine_b + distance, blk)
        return pltpu.make_async_remote_copy(
            src_ref=scores_ref.at[:, pl.ds(pl.multiple_of(target * owned, LANES), owned)],
            dst_ref=gathered.at[mine_b],
            send_sem=score_send.at[distance],
            recv_sem=score_recv.at[distance],
            device_id={"blk": target},
            device_id_type=MESH,
        )

    def score_chunk(distance):
        target = lax.rem(mine_b + distance, blk)
        rows = pl.ds(pl.multiple_of(target * owned, LANES), owned)
        each = lax.dot_general(
            masked_ridge[...], geno[rows, :], (((1,), (1,)), ((), ())),
            preferred_element_type=jnp.float32,
        )
        cohort = cohort_ref[:, rows]
        chosen = each[:8]
        for index in range(1, cohort_count):
            chosen = jnp.where(cohort == index, each[index * 8 : index * 8 + 8], chosen)
        scores_ref[:, rows] = chosen[:per_block] * scale

    def score_step(distance, _):
        score_chunk(distance)
        score_copy(distance).start()
        return 0

    lax.fori_loop(1, blk, score_step, 0)
    score_chunk(0)
    copies = [score_copy(distance) for distance in range(1, blk)]
    own = pl.ds(pl.multiple_of(mine_b * owned, LANES), owned)
    gathered[mine_b] = scores_ref[:, own]
    labels = pheno_ref[:, own].astype(jnp.float32)
    train = (fold_ref[:, own] != 0).astype(jnp.float32)
    for copy in copies:
        copy.wait_recv()
    for block in range(blk):
        packed[block * per_block : (block + 1) * per_block, :] = gathered[block]
    scores = packed[...]
    pieces[...] = jnp.concatenate([scores, low_part(scores)], axis=0).astype(jnp.bfloat16)
    for copy in copies:
        copy.wait_send()

    width = pack_plan(predictors)[3]
    pad_row = lax.broadcasted_iota(jnp.int32, (width - predictors, owned), 0)
    row_of = lax.broadcasted_iota(jnp.int32, (predictors, width), 0)
    column_of = lax.broadcasted_iota(jnp.int32, (predictors, width), 1)
    ridge = level_ridge * total_samples

    def predict(level):
        return jnp.sum(
            packed[...] * jnp.concatenate([level] * (owned // LANES), axis=1), axis=0, keepdims=True
        )

    def widen(level):
        return jnp.concatenate([level] * pl.cdiv(width, LANES), axis=1)[:, :width]

    def newton(step, level):
        prob = jax.nn.sigmoid(predict(level))
        resid = train * (labels - prob)
        curve = train * prob * (1.0 - prob)
        right = jnp.concatenate(
            [packed[...] * curve, jnp.where(pad_row == 0, resid, 0.0)], axis=0
        )
        moments = jnp.zeros((2 * predictors, width), jnp.float32)
        for part in (right, low_part(right)):
            moments = moments + lax.dot_general(
                pieces[...], part.astype(jnp.bfloat16), (((1,), (1,)), ((), ())),
                preferred_element_type=jnp.float32,
            )
        smp_part[step, mine_s] = pack_rows(moments[:predictors] + moments[predictors:])
        over_smp = exchange(
            smp_part.at[step], mine_s, "smp", smp, smp_send.at[step], smp_recv.at[step]
        )
        blk_part[step, mine_b] = over_smp
        system = exchange(
            blk_part.at[step], mine_b, "blk", blk, blk_send.at[step], blk_recv.at[step]
        )
        system = unpack_rows(system, predictors)
        system = jnp.where(row_of == column_of, system + ridge, system)
        system = jnp.where(column_of == predictors, system - ridge * widen(level), system)
        return level + spd_solve(system, predictors)

    level = lax.fori_loop(0, NEWTON, newton, jnp.zeros((predictors, LANES), jnp.float32))
    linear_ref[...] = predict(level)
    diagonal = row_of == column_of
    level_ref[...] = jnp.sum(jnp.where(diagonal, widen(level), 0.0), axis=0, keepdims=True)[
        :, :predictors
    ]


def on_device(genotype, presence, cohort_id, fold_id, phenotype):
    blk = lax.axis_size("blk")
    smp = lax.axis_size("smp")
    local_count, block_width = genotype.shape
    total_samples = local_count * smp
    per_block = len(penalty_list)
    owned = local_count // blk
    predictors = per_block * blk
    system_rows, system_lanes = pack_plan(predictors)[2:]
    cohort_count = presence.shape[0]
    half = gram_rows(block_width) // 2
    size = half // PARTS
    chips = smp // 2
    dma = pltpu.SemaphoreType.DMA
    vmem = pl.BlockSpec(memory_space=pltpu.VMEM)
    level, linear = pl.pallas_call(
        functools.partial(whole_kernel, blk, smp, total_samples, cohort_count),
        out_shape=(
            jax.ShapeDtypeStruct((1, predictors), jnp.float32),
            jax.ShapeDtypeStruct((1, owned), jnp.float32),
        ),
        in_specs=[pl.BlockSpec(memory_space=pl.ANY)] + [vmem] * 4,
        out_specs=(vmem,) * 2,
        scratch_shapes=[
            pltpu.VMEM((local_count, block_width), jnp.bfloat16),
            pltpu.VMEM((8, block_width), jnp.float32),
            pltpu.VMEM((2 * half, TILE), jnp.float32),
            pltpu.VMEM((PARTS, size, TILE), jnp.float32),
            pltpu.VMEM((chips, PARTS, size, TILE), jnp.float32),
            pltpu.VMEM((2 * half, TILE), jnp.float32),
            pltpu.VMEM((2, block_width, block_width), jnp.bfloat16),
            pltpu.VMEM((8 * cohort_count, block_width), jnp.bfloat16),
            pltpu.VMEM((per_block, local_count), jnp.float32),
            pltpu.VMEM((blk, per_block, owned), jnp.float32),
            pltpu.VMEM((predictors, owned), jnp.float32),
            pltpu.VMEM((2 * predictors, owned), jnp.bfloat16),
            pltpu.VMEM((NEWTON, smp, system_rows, system_lanes), jnp.float32),
            pltpu.VMEM((NEWTON, blk, system_rows, system_lanes), jnp.float32),
            dma((local_count // CHUNK,)),
            dma((PARTS,)), dma((PARTS,)),
            dma((chips, PARTS)), dma((chips, PARTS)),
            dma((PARTS,)), dma((PARTS,)),
            dma((blk,)), dma((blk,)),
            dma((NEWTON, smp)), dma((NEWTON, smp)),
            dma((NEWTON, blk)), dma((NEWTON, blk)),
        ],
        compiler_params=pltpu.CompilerParams(
            collective_id=0, has_side_effects=True, vmem_limit_bytes=56 * 1024 * 1024
        ),
    )(
        genotype, presence, cohort_id.reshape(1, -1), fold_id.reshape(1, -1),
        phenotype.reshape(1, -1),
    )
    return level.reshape(predictors), linear.reshape(owned)


def solution(mesh):
    in_specs = (P("smp", "blk"), P(None, "blk"), P("smp"), P("smp"), P("smp"))
    out_specs = (P(), P(("smp", "blk")))
    return jax.shard_map(
        on_device, mesh=mesh, in_specs=in_specs, out_specs=out_specs, check_vma=False
    )
```
